256 devices in a mesh: seq: 64 (over y_lo, x, z), mp: 4 (over y_hi, core).
Axes of the slice: x: 4, y: 4 (y_hi: 2, y_lo: 2; y = y_hi * 2 + y_lo), z: 8, core: 2. Of those that a mesh axis runs over, the one named last changes fastest.
Arguments:
- projected: bfloat16 [3, 4096, 16384], P(None, 'mp', 'seq'), may hold values from -6 to 6
- short_taps: float32 [3, 3, 4096], P(None, None, 'mp'), may hold values from -3.5 to 3.5
- long_filter: bfloat16 [4096, 16384], P('mp', 'seq'), may hold values from -0.046875 to 0.046875
- skip_gain: float32 [4096], P('mp'), may hold values from -4 to 4
- w_out: bfloat16 [4096, 4096], P(None, 'mp'), may hold values from -0.09375 to 0.09375
Outputs:
- mixed: bfloat16 [16384, 4096], P('seq', 'mp')
The draws below stay inside these ranges and needn't reach their ends.
All inputs are finite; a program needn't handle non-finite values.
Results may differ from the reference program's by a relative error of at most 0.0081.
Values may be sent and summed in bfloat16 or wider, within the bound.
No kernel may reach another device: no remote copies, remote signals or barrier semaphores. Data moves between devices by JAX's collectives and lax.ppermute only.
A program may use at most 128 MiB of HBM per device.

```python
import jax
import jax.numpy as jnp
from jax import lax

C = 4096
E = 4096
L = 16384


def block_scale(own_key, dims, cuts, smallest, high):
    loudness = 1.0
    for dim, blocks in cuts:
        steps = jax.random.uniform(jax.random.fold_in(jax.random.fold_in(own_key, 6), dim), (blocks,), jnp.float32, smallest / len(cuts), high / len(cuts))
        loudness = loudness * jnp.repeat(jnp.exp(steps), dims[dim] // blocks).reshape((-1,) + (1,) * (len(dims) - 1 - dim))
    return loudness


def bell_draw(own_key, extent, deviation, bound, shards=(), dtype=jnp.bfloat16):
    array = deviation * jax.random.normal(own_key, extent, jnp.float32)
    if shards:
        array = array * block_scale(own_key, extent, shards, -0.22, 0.18)
    return jnp.clip(array, -bound, bound).astype(dtype)


def setup_inputs(seed: int = 0) -> dict:
    splits = jax.random.split(jax.random.key(seed), 6)
    projected = bell_draw(splits[0], (3, C, L), 1.0, 6.0, ((1, 4), (2, 64)))
    short_taps = bell_draw(splits[1], (3, 3, C), 3 ** -0.5, 3.5, ((2, 4),), jnp.float32)
    long_filter = bell_draw(splits[2], (C, L), L ** -0.5, 0.046875, ((0, 4), (1, 64)))
    skip_gain = bell_draw(splits[3], (C,), 1.0, 4.0, ((0, 4),), jnp.float32)
    w_out = bell_draw(splits[4], (C, E), C ** -0.5, 0.09375, ((1, 4),))
    return dict(projected=projected, short_taps=short_taps, long_filter=long_filter, skip_gain=skip_gain, w_out=w_out)


def featurize(projected, short_taps):
    values = projected.astype(jnp.float32)
    seq_len = values.shape[2]
    padded = jnp.pad(values, ((0, 0), (0, 0), (2, 0)))
    result = short_taps[:, 0, :, None] * padded[:, :, 2:]
    result = result + short_taps[:, 1, :, None] * padded[:, :, 1:seq_len + 1]
    result = result + short_taps[:, 2, :, None] * padded[:, :, 0:seq_len]
    return result.astype(jnp.bfloat16)


def long_block(inputs):
    gated_block, filter_block, skip_block = inputs
    seq_len = gated_block.shape[1]
    signal = gated_block.astype(jnp.float32)
    kernel = filter_block.astype(jnp.float32)
    full_length = 2 * seq_len
    spectrum = jnp.fft.rfft(signal, n=full_length, axis=1) * jnp.fft.rfft(kernel, n=full_length, axis=1)
    convolved = jnp.fft.irfft(spectrum, n=full_length, axis=1)[:, :seq_len]
    return (convolved + skip_block[:, None] * signal).astype(jnp.bfloat16)


def reference(projected, short_taps, long_filter, skip_gain, w_out):
    features = featurize(projected, short_taps)
    gated_kv = (features[1].astype(jnp.float32) * features[2].astype(jnp.float32)).astype(jnp.bfloat16)
    channels = gated_kv.shape[0]
    block_size = 64
    groups = channels // block_size
    response = lax.map(long_block, (gated_kv.reshape(groups, block_size, -1), long_filter.reshape(groups, block_size, -1), skip_gain.reshape(groups, block_size)))
    response = response.reshape(channels, -1)
    product = (features[0].astype(jnp.float32) * response.astype(jnp.float32)).astype(jnp.bfloat16)
    mixed_out = jnp.dot(product.T, w_out, preferred_element_type=jnp.float32)
    return mixed_out.astype(jnp.bfloat16)
```

```python
import jax
import jax.numpy as jnp
import ml_dtypes
import numpy as np
from jax import lax
from jax.experimental import pallas as pl
from jax.experimental.pallas import tpu as pltpu
from jax.sharding import PartitionSpec as P

N1 = 128
N2 = 128


def split(table):
    high = table.astype(ml_dtypes.bfloat16)
    low = (table - high.astype(np.float64)).astype(ml_dtypes.bfloat16)
    return high, low


def dft_tables(rows):
    order = np.concatenate([np.arange(0, N1, 2), np.arange(1, N1, 2)])
    k1 = np.arange(N1)
    first = 2.0 * np.pi * np.outer(k1 + 0.25, order) / N1
    stage1 = np.concatenate([np.cos(first), -np.sin(first)], axis=0)
    s1_hi, s1_lo = split(stage1)
    stage1 = np.concatenate([s1_hi, s1_lo], axis=1)
    turn = 2.0 * np.pi * np.outer(k1 + 0.25, np.arange(N2)) / (N1 * N2)
    turns = np.stack([np.cos(turn), np.sin(turn)]).astype(np.float32)
    second = 2.0 * np.pi * np.outer(np.arange(N2), np.arange(N2)) / N2
    cos, sin = np.cos(second), np.sin(second)
    forward2 = np.stack(split(np.block([[cos, -sin], [sin, cos]])))
    inverse2 = np.stack(split(np.block([[cos, sin], [-sin, cos]])))
    last = np.concatenate([np.cos(first.T), -np.sin(first.T)], axis=1) / (N1 * N2)
    inverse1 = np.concatenate(split(last), axis=0)
    return stage1, turns, forward2, inverse2, inverse1


def dot(a, b):
    return jnp.dot(a, b, preferred_element_type=jnp.float32)


def halves(value):
    high = value.astype(jnp.bfloat16)
    low = (value - high.astype(jnp.float32)).astype(jnp.bfloat16)
    return high, low


def wide_dot(value, table):
    high, low = halves(value)
    return dot(high, table[0]) + (dot(high, table[1]) + dot(low, table[0]))


def load_tile(flat, channel, parts, per_dev):
    picked = [
        half[pl.ds(channel, parts, stride=per_dev), :] for half in flat
    ]
    return jnp.concatenate(picked, axis=0)


def unpack(source, flat, parts, per_dev):
    for half in range(2):
        flat[half][...] = (
            source[:, :, half * N2 : (half + 1) * N2]
            .astype(jnp.float32)
            .reshape(parts * per_dev, N2)
        )


def spectrum_of(tiles, stage1, turns, forward2):
    pair = jnp.concatenate([tile.astype(jnp.bfloat16) for tile in tiles], axis=1)
    both = dot(stage1[...], jnp.concatenate([pair, pair], axis=0))
    cos, sin = turns[0], turns[1]
    result = []
    for place in range(len(tiles)):
        re = both[:N1, place * N2 : (place + 1) * N2]
        im = both[N1:, place * N2 : (place + 1) * N2]
        turned = jnp.concatenate([re * cos + im * sin, im * cos - re * sin], axis=1)
        result.append(wide_dot(turned, (forward2[0], forward2[1])))
    return result


def filter_kernel(received, stage1, turns, forward2, spectrum, even, odd):
    parts, per_dev, _ = received.shape
    flat = (even, odd)
    unpack(received, flat, parts, per_dev)
    for first in range(0, per_dev, 2):
        tiles = [load_tile(flat, first + place, parts, per_dev) for place in range(2)]
        for place, result in enumerate(spectrum_of(tiles, stage1, turns, forward2)):
            spectrum[first + place] = result


def conv_kernel(
    received, spectrum, skip, stage1, turns, forward2, inverse2, inverse1, response, even, odd
):
    parts, per_dev, _ = received.shape
    flat = (even, odd)
    unpack(received, flat, parts, per_dev)
    cos, sin = turns[0], turns[1]
    for first in range(0, per_dev, 2):
        tiles = [load_tile(flat, first + place, parts, per_dev) for place in range(2)]
        spectra = spectrum_of(tiles, stage1, turns, forward2)
        turned_back = []
        for place in range(2):
            sig_re, sig_im = spectra[place][:, :N2], spectra[place][:, N2:]
            ker = spectrum[first + place]
            ker_re, ker_im = ker[:, :N2], ker[:, N2:]
            prod = jnp.concatenate(
                [sig_re * ker_re - sig_im * ker_im, sig_re * ker_im + sig_im * ker_re], axis=1
            )
            back = wide_dot(prod, (inverse2[0], inverse2[1]))
            re, im = back[:, :N2], back[:, N2:]
            turned_back.append(
                jnp.concatenate([re * cos - im * sin, re * sin + im * cos], axis=0)
            )
        high, low = halves(jnp.concatenate(turned_back, axis=1))
        most = dot(inverse1[...], high)
        restored = most[:N1] + (most[N1:] + dot(inverse1[:N1, :], low))
        for place in range(2):
            out = restored[:, place * N2 : (place + 1) * N2] + skip[first + place] * tiles[place]
            for half in range(2):
                flat[half][pl.ds(first + place, parts, stride=per_dev), :] = out[
                    half * parts : (half + 1) * parts
                ]
    for half in range(2):
        response[:, :, half * N2 : (half + 1) * N2] = (
            flat[half][...].reshape(parts, per_dev, N2).astype(jnp.bfloat16)
        )


def call(kernel, out_shape, args, specs, scratch, flops, moved):
    return pl.pallas_call(
        kernel,
        out_shape=out_shape,
        in_specs=specs,
        out_specs=pl.BlockSpec(memory_space=pltpu.VMEM),
        scratch_shapes=scratch,
        compiler_params=pltpu.CompilerParams(vmem_limit_bytes=32 * 2**20),
        cost_estimate=pl.CostEstimate(flops=flops, bytes_accessed=moved, transcendentals=0),
    )(*args)


def whole():
    return pl.BlockSpec(memory_space=pltpu.VMEM)


def per_device(projected, short_taps, long_filter, skip_gain, w_out):
    tok_len = projected.shape[2]
    quarter = projected.shape[1]
    seq_parts = lax.axis_size("seq")
    per_dev = quarter // seq_parts
    chunks = (seq_parts, per_dev, tok_len)
    stage1, turns, forward2, inverse2, inverse1 = [jnp.asarray(t) for t in dft_tables(seq_parts)]

    filter_in = lax.all_to_all(long_filter.reshape(chunks), "seq", split_axis=0, concat_axis=0, tiled=True)

    rim = projected[:, :, tok_len - 2 :]
    before = lax.ppermute(rim, "seq", [(s, s + 1) for s in range(seq_parts - 1)])
    joined = jnp.concatenate([before, projected], axis=2).astype(jnp.float32)
    features = short_taps[:, 0, :, None] * joined[:, :, 2:]
    features = features + short_taps[:, 1, :, None] * joined[:, :, 1 : tok_len + 1]
    features = (features + short_taps[:, 2, :, None] * joined[:, :, 0:tok_len]).astype(jnp.bfloat16)
    gated = (features[1].astype(jnp.float32) * features[2].astype(jnp.float32)).astype(jnp.bfloat16)
    signal_in = lax.all_to_all(gated.reshape(chunks), "seq", split_axis=0, concat_axis=0, tiled=True)

    scratch = [pltpu.VMEM((seq_parts * per_dev, N2), jnp.float32) for _ in range(2)]
    spectrum = call(
        filter_kernel,
        jax.ShapeDtypeStruct((per_dev, N1, 2 * N2), jnp.float32),
        (filter_in, stage1, turns, forward2),
        [whole()] * 4,
        scratch,
        2_000_000_000,
        4_000_000,
    )
    own_skip = lax.dynamic_slice_in_dim(skip_gain, lax.axis_index("seq") * per_dev, per_dev, 0)
    response = call(
        conv_kernel,
        jax.ShapeDtypeStruct(chunks, jnp.bfloat16),
        (signal_in, spectrum, own_skip, stage1, turns, forward2, inverse2, inverse1),
        [whole(), whole(), pl.BlockSpec(memory_space=pltpu.SMEM)] + [whole()] * 5,
        scratch,
        4_000_000_000,
        4_000_000,
    )
    returned = lax.all_to_all(response, "seq", split_axis=0, concat_axis=0, tiled=True)
    product = (
        features[0].astype(jnp.float32) * returned.reshape(quarter, tok_len).astype(jnp.float32)
    ).astype(jnp.bfloat16)

    me = lax.axis_index("mp")
    far = lax.ppermute(product, "mp", [(m, m ^ 2) for m in range(4)])
    near = lax.ppermute(product, "mp", [(m, m ^ 1) for m in range(4)])

    def part(value, flip):
        rows = lax.dynamic_slice_in_dim(w_out, (me ^ flip) * quarter, quarter, 0)
        return lax.dot_general(
            value, rows, (((0,), (0,)), ((), ())), preferred_element_type=jnp.float32
        )

    total = part(product, 0) + part(near, 1)
    last = lax.ppermute(far, "mp", [(m, m ^ 1) for m in range(4)])
    total = total + part(far, 2) + part(last, 3)
    return total.astype(jnp.bfloat16)


def solution(mesh):
    return jax.shard_map(
        per_device,
        mesh=mesh,
        in_specs=(
            P(None, "mp", "seq"),
            P(None, None, "mp"),
            P("mp", "seq"),
            P("mp"),
            P(None, "mp"),
        ),
        out_specs=P("seq", "mp"),
        check_vma=False,
    )
```

```python
import jax
import jax.numpy as jnp
import ml_dtypes
import numpy as np
from jax import lax
from jax.experimental import pallas as pl
from jax.experimental.pallas import tpu as pltpu
from jax.sharding import PartitionSpec as P

N1 = 128
N2 = 128
GROUP = 8
STRIP = 64


def split(table):
    high = table.astype(ml_dtypes.bfloat16)
    low = (table - high.astype(np.float64)).astype(ml_dtypes.bfloat16)
    return high, low


def dft_tables():
    order = np.concatenate([np.arange(0, N1, 2), np.arange(1, N1, 2)])
    k1 = np.arange(N1)
    first = 2.0 * np.pi * np.outer(k1 + 0.25, order) / N1
    stage1 = np.concatenate(split(np.concatenate([np.cos(first), -np.sin(first)], axis=0)), axis=1)
    turn = 2.0 * np.pi * np.outer(k1 + 0.25, np.arange(N2)) / (N1 * N2)
    turns = np.stack([np.cos(turn), np.sin(turn)]).astype(np.float32)
    second = 2.0 * np.pi * np.outer(np.arange(N2), np.arange(N2)) / N2
    cos, sin = np.cos(second), np.sin(second)
    high, low = split(np.block([[cos, -sin], [sin, cos]]))
    forward2 = np.concatenate([high, high, low], axis=0)
    high, low = split(np.block([[cos, sin], [-sin, cos]]))
    inverse2 = np.concatenate([high, high, low], axis=0)
    last = np.concatenate([np.cos(first.T), -np.sin(first.T)], axis=1) / (N1 * N2)
    inverse1 = np.concatenate(split(last), axis=0)
    return stage1, turns, forward2, inverse2, inverse1


def dot(a, b):
    return jnp.dot(a, b, preferred_element_type=jnp.float32)


def halves(value):
    high = value.astype(jnp.bfloat16)
    low = (value - high.astype(jnp.float32)).astype(jnp.bfloat16)
    return high, low


def wide_dot(value, table):
    high, low = halves(value)
    return dot(jnp.concatenate([high, low, high], axis=1), table)


def load_tile(flat, row, parts, stride):
    return jnp.concatenate([half[pl.ds(row, parts, stride=stride), :] for half in flat], axis=0)


def spectra_of(tiles, stage1, turns, forward2):
    cos, sin = turns[0], turns[1]
    turned = []
    for first in range(0, len(tiles), 2):
        pair = jnp.concatenate(tiles[first : first + 2], axis=1).astype(jnp.bfloat16)
        both = dot(stage1[...], jnp.concatenate([pair, pair], axis=0))
        for place in range(2):
            re = both[:N1, place * N2 : (place + 1) * N2]
            im = both[N1:, place * N2 : (place + 1) * N2]
            turned.append(jnp.concatenate([re * cos + im * sin, im * cos - re * sin], axis=1))
    return wide_dot(jnp.concatenate(turned, axis=0), forward2[...])


def conv_kernel(
    received, skip, stage1, turns, forward2, inverse2, inverse1, response,
    even, odd, out_even, out_odd, product, spectrum,
):
    parts, rows, _ = received.shape
    per_dev = rows // 2
    flat, out_flat = (even, odd), (out_even, out_odd)
    for half in range(2):
        flat[half][...] = (
            received[:, :, half * N2 : (half + 1) * N2].astype(jnp.float32).reshape(parts * rows, N2)
        )
    for start, spectra in ((per_dev, spectrum), (0, product)):
        for first in range(0, per_dev, GROUP):
            tiles = [load_tile(flat, start + first + c, parts, rows) for c in range(GROUP)]
            spectra[first * N1 : (first + GROUP) * N1, :] = spectra_of(tiles, stage1, turns, forward2)
    cos, sin = turns[0], turns[1]
    for first in range(0, per_dev, GROUP):
        span = slice(first * N1, (first + GROUP) * N1)
        sig_re, sig_im = product[span, :N2], product[span, N2:]
        ker_re, ker_im = spectrum[span, :N2], spectrum[span, N2:]
        multiplied = jnp.concatenate(
            [sig_re * ker_re - sig_im * ker_im, sig_re * ker_im + sig_im * ker_re], axis=1
        )
        back = wide_dot(multiplied, inverse2[...])
        for c in range(0, GROUP, 2):
            turned = []
            for place in (c, c + 1):
                re = back[place * N1 : (place + 1) * N1, :N2]
                im = back[place * N1 : (place + 1) * N1, N2:]
                turned.append(jnp.concatenate([re * cos - im * sin, re * sin + im * cos], axis=0))
            high, low = halves(jnp.concatenate(turned, axis=1))
            most = dot(inverse1[...], high)
            restored = most[:N1] + (most[N1:] + dot(inverse1[:N1, :], low))
            for place in range(2):
                channel = first + c + place
                tile = load_tile(flat, channel, parts, rows)
                out = restored[:, place * N2 : (place + 1) * N2] + skip[channel : channel + 1, :] * tile
                for half in range(2):
                    out_flat[half][pl.ds(channel, parts, stride=per_dev), :] = out[
                        half * parts : (half + 1) * parts
                    ]
    for half in range(2):
        response[:, :, half * N2 : (half + 1) * N2] = (
            out_flat[half][...].reshape(parts, per_dev, N2).astype(jnp.bfloat16)
        )


def tap_columns(taps, cols):
    rows = [taps[group] for group in range(3)] + [jnp.zeros((7, taps.shape[2]), jnp.float32)]
    columns = jnp.concatenate([row[:, cols] for row in rows], axis=0).T
    return [[columns[:, 3 * g + p : 3 * g + p + 1] for p in range(3)] for g in range(3)]


def weigh(tap, value, back1, back2):
    return (tap[0] * value + tap[1] * back1 + tap[2] * back2).astype(jnp.bfloat16)


def short_feature(left, right, tap, older, newer):
    left, right = left.astype(jnp.float32), right.astype(jnp.float32)
    lane = lax.broadcasted_iota(jnp.int32, left.shape, 1)
    left1, left2 = pltpu.roll(left, 1, 1), pltpu.roll(left, 2, 1)
    right1 = jnp.where(lane < 1, left1, pltpu.roll(right, 1, 1))
    right2 = jnp.where(lane < 2, left2, pltpu.roll(right, 2, 1))
    left1 = jnp.where(lane < 1, newer, left1)
    left2 = jnp.where(lane < 1, older, jnp.where(lane < 2, newer, left2))
    return weigh(tap, left, left1, left2), weigh(tap, right, right1, right2)


def gate(k, v):
    return (k.astype(jnp.float32) * v.astype(jnp.float32)).astype(jnp.bfloat16)


def strips(channels):
    return [slice(first, first + STRIP) for first in range(0, channels, STRIP)]


def edge_rows(pick, tiles):
    return [
        lax.dot_general(pick, tile, (((1,), (1,)), ((), ())), preferred_element_type=jnp.float32)
        for tile in tiles
    ]


def picker(lanes):
    row = lax.broadcasted_iota(jnp.int32, (16, N2), 0)
    lane = lax.broadcasted_iota(jnp.int32, (16, N2), 1)
    hit = jnp.zeros((16, N2), jnp.bool_)
    for place, wanted in enumerate(lanes):
        hit = hit | ((row == place) & (lane == wanted))
    return jnp.where(hit, 1.0, 0.0).astype(jnp.bfloat16)


def rim_kernel(projected, long_filter, short_taps, tails, pair, filter_out, taps, edge, arrived):
    groups, channels, _ = edge.shape
    moves = (
        (projected.at[:, :, N2:], edge),
        (projected.at[1:], pair),
        (long_filter, filter_out),
        (short_taps, taps),
    )
    copies = [
        pltpu.make_async_copy(source, target, arrived.at[place])
        for place, (source, target) in enumerate(moves)
    ]
    for copy in copies:
        copy.start()
    copies[0].wait()
    rows = edge_rows(picker((N2 - 2, N2 - 1)), [edge[group] for group in range(groups)])
    picked = [t[place : place + 1] for place in range(2) for t in rows]
    picked.append(jnp.zeros((2, channels), jnp.float32))
    tails[...] = jnp.concatenate(picked, axis=0).astype(jnp.bfloat16)
    for copy in copies[1:]:
        copy.wait()


def gate_kernel(pair, taps, gated, heads):
    _, channels, _ = pair.shape
    for first in range(0, channels, N1):
        columns = tap_columns(taps, slice(first, first + N1))
        for rows in strips(N1):
            place = slice(first + rows.start, first + rows.stop)
            k, v = [
                short_feature(
                    pair[group - 1, place, :N2],
                    pair[group - 1, place, N2:],
                    [column[rows] for column in columns[group]],
                    0.0,
                    0.0,
                )
                for group in (1, 2)
            ]
            gated[place, :N2] = gate(k[0], v[0])
            gated[place, N2:] = gate(k[1], v[1])
    rows = edge_rows(picker((0, 1)), [pair[group, :, :N2] for group in range(2)])
    picked = [t[place : place + 1] for place in range(2) for t in rows]
    picked.append(jnp.zeros((4, channels), jnp.float32))
    heads[...] = jnp.concatenate(picked, axis=0)


def mend_kernel(started, taps, rims, heads, long_filter, send):
    channels, tok_len = started.shape
    dests, sent, _ = send.shape
    per_dev = sent // 2
    ends = []
    for group in (1, 2):
        tap = [taps[group, place : place + 1, :] for place in range(3)]
        older = rims[group : group + 1, :].astype(jnp.float32)
        newer = rims[3 + group : 4 + group, :].astype(jnp.float32)
        zero, one = heads[group - 1 : group, :], heads[1 + group : 2 + group, :]
        ends.append(
            (
                (tap[0] * zero + tap[1] * newer + tap[2] * older).astype(jnp.bfloat16),
                (tap[0] * one + tap[1] * zero + tap[2] * newer).astype(jnp.bfloat16),
            )
        )
    first, second = [gate(k, v).astype(jnp.float32) for k, v in zip(*ends)]
    lane = lax.broadcasted_iota(jnp.int32, (N1, N2), 1)
    row = lax.broadcasted_iota(jnp.int32, (N1, N2), 0)
    for start in range(0, channels, N1):
        cols = slice(start, start + N1)
        to = slice(start // per_dev, (start + N1) // per_dev)
        spread = jnp.where(row == 0, first[:, cols], second[:, cols])
        value = started[cols, :N2].astype(jnp.float32)
        mended = jnp.where(lane < 2, spread.T, value).astype(jnp.bfloat16)
        send[to, :per_dev, :N2] = mended.reshape(N1 // per_dev, per_dev, N2)
    send[:, :per_dev, N2:] = started[:, N2:].reshape(dests, per_dev, tok_len - N2)
    send[:, per_dev:, :] = long_filter[...].reshape(dests, per_dev, tok_len)


def query_kernel(projected, taps, rims, query, held, arrived):
    channels, _ = held.shape
    copy = pltpu.make_async_copy(projected.at[0], held, arrived)
    copy.start()
    copy.wait()
    for first in range(0, channels, N1):
        cols = slice(first, first + N1)
        tap = tap_columns(taps, cols)[0]
        rims_t = jnp.concatenate(
            [rims[:, cols].astype(jnp.float32), jnp.zeros((8, N1), jnp.float32)], axis=0
        ).T
        for rows in strips(N1):
            place = slice(first + rows.start, first + rows.stop)
            query[place, :N2], query[place, N2:] = short_feature(
                held[place, :N2],
                held[place, N2:],
                [column[rows] for column in tap],
                rims_t[rows, 0:1],
                rims_t[rows, 3:4],
            )


def product_kernel(query, returned, turned):
    product = query[...].astype(jnp.float32) * returned[...].astype(jnp.float32)
    turned[...] = product.T.astype(jnp.bfloat16)


def own_matmul_kernel(mine, w_out, total, rest, held, arrived):
    me = lax.axis_index("mp")
    quarter = mine.shape[1]
    copies = []
    for flip in range(4):
        rows = pl.ds(pl.multiple_of((me ^ flip) * quarter, quarter), quarter)
        target = rest.at[pl.ds((flip - 1) * quarter, quarter), :] if flip else held
        copy = pltpu.make_async_copy(w_out.at[rows, :], target, arrived.at[flip])
        copy.start()
        copies.append(copy)
    copies[0].wait()
    total[...] = dot(mine[...], held[...])
    for copy in copies[1:]:
        copy.wait()


def cost(flops, moved):
    return pl.CostEstimate(flops=flops, bytes_accessed=moved, transcendentals=0)


def whole():
    return pl.BlockSpec(memory_space=pltpu.VMEM)


def in_hbm(value):
    return pltpu.with_memory_space_constraint(value, pltpu.HBM)


PARAMS = pltpu.CompilerParams(vmem_limit_bytes=32 * 2**20)


def per_device(projected, short_taps, long_filter, skip_gain, w_out):
    tok_len = projected.shape[2]
    quarter = projected.shape[1]
    seq_parts = lax.axis_size("seq")
    per_dev = quarter // seq_parts
    chunk = (seq_parts, per_dev, tok_len)
    stage1, turns, forward2, inverse2, inverse1 = [jnp.asarray(table) for table in dft_tables()]
    projected = in_hbm(projected)
    anywhere = pl.BlockSpec(memory_space=pl.ANY)

    def transposed(value):
        return lax.all_to_all(value, "seq", split_axis=0, concat_axis=0, tiled=True)

    tails, pair, filter_here, taps = pl.pallas_call(
        rim_kernel,
        out_shape=[
            jax.ShapeDtypeStruct((8, quarter), jnp.bfloat16),
            jax.ShapeDtypeStruct((2, quarter, tok_len), jnp.bfloat16),
            jax.ShapeDtypeStruct((quarter, tok_len), jnp.bfloat16),
            jax.ShapeDtypeStruct(short_taps.shape, jnp.float32),
        ],
        in_specs=[anywhere] * 3,
        out_specs=[whole()] * 4,
        scratch_shapes=[
            pltpu.VMEM((3, quarter, N2), jnp.bfloat16),
            pltpu.SemaphoreType.DMA((4,)),
        ],
        compiler_params=PARAMS,
        cost_estimate=cost(1000, 1000),
    )(projected, in_hbm(long_filter), in_hbm(short_taps))
    rims = lax.ppermute(tails, "seq", [(s, s + 1) for s in range(seq_parts - 1)])
    started, heads = pl.pallas_call(
        gate_kernel,
        out_shape=[
            jax.ShapeDtypeStruct((quarter, tok_len), jnp.bfloat16),
            jax.ShapeDtypeStruct((8, quarter), jnp.float32),
        ],
        in_specs=[whole()] * 2,
        out_specs=[whole()] * 2,
        compiler_params=PARAMS,
        cost_estimate=cost(1000, 1000),
    )(pair, taps)
    send = pl.pallas_call(
        mend_kernel,
        out_shape=jax.ShapeDtypeStruct((seq_parts, 2 * per_dev, tok_len), jnp.bfloat16),
        in_specs=[whole()] * 5,
        out_specs=whole(),
        compiler_params=PARAMS,
        cost_estimate=cost(1000, 1000),
    )(started, taps, rims, heads, filter_here)
    received = transposed(send)
    query = pl.pallas_call(
        query_kernel,
        out_shape=jax.ShapeDtypeStruct((quarter, tok_len), jnp.bfloat16),
        in_specs=[anywhere, whole(), whole()],
        out_specs=whole(),
        scratch_shapes=[pltpu.VMEM((quarter, tok_len), jnp.bfloat16), pltpu.SemaphoreType.DMA],
        compiler_params=PARAMS,
        cost_estimate=cost(5_000_000, 1_000_000),
    )(projected, taps, rims)
    received, query = lax.optimization_barrier((received, query))

    own_skip = lax.dynamic_slice_in_dim(skip_gain, lax.axis_index("seq") * per_dev, per_dev, 0)
    own_skip = jnp.broadcast_to(own_skip[:, None], (per_dev, N2))
    response = pl.pallas_call(
        conv_kernel,
        out_shape=jax.ShapeDtypeStruct(chunk, jnp.bfloat16),
        in_specs=[whole()] * 7,
        out_specs=whole(),
        scratch_shapes=[pltpu.VMEM((2 * quarter, N2), jnp.float32) for _ in range(2)]
        + [pltpu.VMEM((quarter, N2), jnp.float32) for _ in range(2)]
        + [pltpu.VMEM((per_dev * N1, 2 * N2), jnp.float32) for _ in range(2)],
        compiler_params=PARAMS,
        cost_estimate=cost(6_000_000_000, 4_000_000),
    )(received, own_skip, stage1, turns, forward2, inverse2, inverse1)
    returned = transposed(response)

    product = pl.pallas_call(
        product_kernel,
        out_shape=jax.ShapeDtypeStruct((tok_len, quarter), jnp.bfloat16),
        in_specs=[whole()] * 2,
        out_specs=whole(),
        compiler_params=PARAMS,
        cost_estimate=cost(1_000_000, 1_500_000),
    )(query, returned.reshape(quarter, tok_len))

    me = lax.axis_index("mp")
    to_far = [(m, m ^ 2) for m in range(4)]
    to_near = [(m, m ^ 1) for m in range(4)]

    far = lax.ppermute(product, "mp", to_far)
    near = lax.ppermute(product, "mp", to_near)
    out_len = w_out.shape[1]
    total, rest = pl.pallas_call(
        own_matmul_kernel,
        out_shape=[
            jax.ShapeDtypeStruct((tok_len, out_len), jnp.float32),
            jax.ShapeDtypeStruct((3 * quarter, out_len), jnp.bfloat16),
        ],
        in_specs=[whole(), anywhere],
        out_specs=[whole()] * 2,
        scratch_shapes=[pltpu.VMEM((quarter, out_len), jnp.bfloat16), pltpu.SemaphoreType.DMA((4,))],
        compiler_params=PARAMS,
        cost_estimate=cost(1000, 1000),
    )(product, in_hbm(w_out))
    total, rest, far = lax.optimization_barrier((total, rest, far))
    last = lax.ppermute(far, "mp", to_near)
    total = total + dot(far, rest[quarter : 2 * quarter])
    total = total + dot(near, rest[:quarter])
    return (total + dot(last, rest[2 * quarter :])).astype(jnp.bfloat16)


def solution(mesh):
    return jax.shard_map(
        per_device,
        mesh=mesh,
        in_specs=(
            P(None, "mp", "seq"),
            P(None, None, "mp"),
            P("mp", "seq"),
            P("mp"),
            P(None, "mp"),
        ),
        out_specs=P("seq", "mp"),
        check_vma=False,
    )
```

```python
import jax
import jax.numpy as jnp
import ml_dtypes
import numpy as np
from jax import lax
from jax.experimental import pallas as pl
from jax.experimental.pallas import tpu as pltpu
from jax.sharding import PartitionSpec as P

N1 = 128
N2 = 128
GROUP = 16
GAP = 8
STRIP = 64


def split(table):
    high = table.astype(ml_dtypes.bfloat16)
    low = (table - high.astype(np.float64)).astype(ml_dtypes.bfloat16)
    return high, low


def dft_tables():
    order = np.concatenate([np.arange(0, N1, 2), np.arange(1, N1, 2)])
    k1 = np.arange(N1)
    first = 2.0 * np.pi * np.outer(k1 + 0.25, order) / N1
    stage1 = np.concatenate(split(np.concatenate([np.cos(first), -np.sin(first)], axis=0)), axis=1)
    turn = 2.0 * np.pi * np.outer(k1 + 0.25, np.arange(N2)) / (N1 * N2)
    turns = np.stack([np.cos(turn), np.sin(turn)]).astype(np.float32)
    second = 2.0 * np.pi * np.outer(np.arange(N2), np.arange(N2)) / N2
    cos, sin = np.cos(second), np.sin(second)
    high, low = split(np.block([[cos, -sin], [sin, cos]]))
    forward2 = np.concatenate([high, high, low], axis=0)
    high, low = split(np.block([[cos, sin], [-sin, cos]]))
    inverse2 = np.concatenate([high, high, low], axis=0)
    last = np.concatenate([np.cos(first.T), -np.sin(first.T)], axis=1) / (N1 * N2)
    inverse1 = np.concatenate(split(last), axis=0)
    return stage1, turns, forward2, inverse2, inverse1


def dot(a, b):
    return jnp.dot(a, b, preferred_element_type=jnp.float32)


def halves(value):
    high = value.astype(jnp.bfloat16)
    low = (value - high.astype(jnp.float32)).astype(jnp.bfloat16)
    return high, low


def wide_dot(value, table):
    high, low = halves(value)
    wide = jnp.concatenate([high, low, high], axis=1)
    middle = wide.shape[0] // 2
    return jnp.concatenate([dot(wide[:middle], table), dot(wide[middle:], table)], axis=0)


def load_tile(flat, row, parts, stride):
    return jnp.concatenate([half[pl.ds(row, parts, stride=stride), :] for half in flat], axis=0)


def spectra_of(tiles, stage1, turns, forward2):
    cos, sin = turns[0], turns[1]
    turned = []
    for first in range(0, len(tiles), 2):
        pair = jnp.concatenate(tiles[first : first + 2], axis=1).astype(jnp.bfloat16)
        both = dot(stage1[...], jnp.concatenate([pair, pair], axis=0))
        for place in range(2):
            re = both[:N1, place * N2 : (place + 1) * N2]
            im = both[N1:, place * N2 : (place + 1) * N2]
            turned.append(jnp.concatenate([re * cos + im * sin, im * cos - re * sin], axis=1))
    return wide_dot(jnp.concatenate(turned, axis=0), forward2[...])


def conv_kernel(
    received, skip, stage1, turns, forward2, inverse2, inverse1, response,
    even, odd, out_even, out_odd, product, spectrum,
):
    parts, rows, _ = received.shape
    per_dev = rows // 2
    flat, out_flat = (even, odd), (out_even, out_odd)
    lanes = [slice(half * N2, (half + 1) * N2) for half in range(2)]
    in_step, out_step = rows + GAP, per_dev + GAP
    for half in range(2):
        for part in range(parts):
            flat[half][part * in_step : part * in_step + rows, :] = received[
                part, :, lanes[half]
            ].astype(jnp.float32)
    for start, spectra in ((per_dev, spectrum), (0, product)):
        for first in range(0, per_dev, GROUP):
            tiles = [load_tile(flat, start + first + c, parts, in_step) for c in range(GROUP)]
            spectra[first * N1 : (first + GROUP) * N1, :] = spectra_of(tiles, stage1, turns, forward2)
    cos, sin = turns[0], turns[1]
    for first in range(0, per_dev, GROUP):
        span = slice(first * N1, (first + GROUP) * N1)
        sig_re, sig_im = product[span, :N2], product[span, N2:]
        ker_re, ker_im = spectrum[span, :N2], spectrum[span, N2:]
        multiplied = jnp.concatenate(
            [sig_re * ker_re - sig_im * ker_im, sig_re * ker_im + sig_im * ker_re], axis=1
        )
        back = wide_dot(multiplied, inverse2[...])
        for c in range(0, GROUP, 2):
            turned = []
            for place in (c, c + 1):
                re = back[place * N1 : (place + 1) * N1, :N2]
                im = back[place * N1 : (place + 1) * N1, N2:]
                turned.append(jnp.concatenate([re * cos - im * sin, re * sin + im * cos], axis=0))
            high, low = halves(jnp.concatenate(turned, axis=1))
            most = dot(inverse1[...], high)
            restored = most[:N1] + (most[N1:] + dot(inverse1[:N1, :], low))
            for place in range(2):
                channel = first + c + place
                out = restored[:, place * N2 : (place + 1) * N2]
                for half in range(2):
                    out_flat[half][pl.ds(channel, parts, stride=out_step), :] = out[
                        half * parts : (half + 1) * parts
                    ]
    for half in range(2):
        for part in range(parts):
            direct = skip[...] * received[part, :per_dev, lanes[half]].astype(jnp.float32)
            convolved = out_flat[half][part * out_step : part * out_step + per_dev, :]
            response[part, :, lanes[half]] = (convolved + direct).astype(jnp.bfloat16)


def tap_columns(taps, cols):
    rows = [taps[group] for group in range(3)] + [jnp.zeros((7, taps.shape[2]), jnp.float32)]
    columns = jnp.concatenate([row[:, cols] for row in rows], axis=0).T
    return [[columns[:, 3 * g + p : 3 * g + p + 1] for p in range(3)] for g in range(3)]


def weigh(tap, value, back1, back2):
    return (tap[0] * value + tap[1] * back1 + tap[2] * back2).astype(jnp.bfloat16)


def short_feature(left, right, tap, older, newer):
    left, right = left.astype(jnp.float32), right.astype(jnp.float32)
    lane = lax.broadcasted_iota(jnp.int32, left.shape, 1)
    left1, left2 = pltpu.roll(left, 1, 1), pltpu.roll(left, 2, 1)
    right1 = jnp.where(lane < 1, left1, pltpu.roll(right, 1, 1))
    right2 = jnp.where(lane < 2, left2, pltpu.roll(right, 2, 1))
    left1 = jnp.where(lane < 1, newer, left1)
    left2 = jnp.where(lane < 1, older, jnp.where(lane < 2, newer, left2))
    return weigh(tap, left, left1, left2), weigh(tap, right, right1, right2)


def gate(k, v):
    return (k.astype(jnp.float32) * v.astype(jnp.float32)).astype(jnp.bfloat16)


def strips(channels):
    return [slice(first, first + STRIP) for first in range(0, channels, STRIP)]


def edge_rows(pick, tiles):
    return [
        lax.dot_general(pick, tile, (((1,), (1,)), ((), ())), preferred_element_type=jnp.float32)
        for tile in tiles
    ]


def picker(lanes):
    row = lax.broadcasted_iota(jnp.int32, (16, N2), 0)
    lane = lax.broadcasted_iota(jnp.int32, (16, N2), 1)
    hit = jnp.zeros((16, N2), jnp.bool_)
    for place, wanted in enumerate(lanes):
        hit = hit | ((row == place) & (lane == wanted))
    return jnp.where(hit, 1.0, 0.0).astype(jnp.bfloat16)


def rim_kernel(projected, long_filter, short_taps, tails, pair, filter_out, taps, edge, arrived):
    groups, channels, _ = edge.shape
    moves = (
        (projected.at[:, :, N2:], edge),
        (projected.at[1:], pair),
        (long_filter, filter_out),
        (short_taps, taps),
    )
    copies = [
        pltpu.make_async_copy(source, target, arrived.at[place])
        for place, (source, target) in enumerate(moves)
    ]
    for copy in copies:
        copy.start()
    copies[0].wait()
    rows = edge_rows(picker((N2 - 2, N2 - 1)), [edge[group] for group in range(groups)])
    picked = [t[place : place + 1] for place in range(2) for t in rows]
    picked.append(jnp.zeros((2, channels), jnp.float32))
    tails[...] = jnp.concatenate(picked, axis=0).astype(jnp.bfloat16)
    for copy in copies[1:]:
        copy.wait()


def gate_kernel(pair, taps, gated, heads):
    _, channels, _ = pair.shape
    for first in range(0, channels, N1):
        columns = tap_columns(taps, slice(first, first + N1))
        for rows in strips(N1):
            place = slice(first + rows.start, first + rows.stop)
            k, v = [
                short_feature(
                    pair[group - 1, place, :N2],
                    pair[group - 1, place, N2:],
                    [column[rows] for column in columns[group]],
                    0.0,
                    0.0,
                )
                for group in (1, 2)
            ]
            gated[place, :N2] = gate(k[0], v[0])
            gated[place, N2:] = gate(k[1], v[1])
    rows = edge_rows(picker((0, 1)), [pair[group, :, :N2] for group in range(2)])
    picked = [t[place : place + 1] for place in range(2) for t in rows]
    picked.append(jnp.zeros((4, channels), jnp.float32))
    heads[...] = jnp.concatenate(picked, axis=0)


def mend_kernel(started, taps, rims, heads, long_filter, send, edge, arrived):
    dests, per_dev, _ = edge.shape
    channels = dests * per_dev
    copies = [
        pltpu.make_async_copy(
            started.reshape(dests, per_dev, 2 * N2).at[:, :, N2:],
            send.at[:, :per_dev, N2:],
            arrived.at[0],
        ),
        pltpu.make_async_copy(
            long_filter.reshape(dests, per_dev, 2 * N2), send.at[:, per_dev:, :], arrived.at[1]
        ),
    ]
    for copy in copies:
        copy.start()
    ends = []
    for group in (1, 2):
        tap = [taps[group, place : place + 1, :] for place in range(3)]
        older = rims[group : group + 1, :].astype(jnp.float32)
        newer = rims[3 + group : 4 + group, :].astype(jnp.float32)
        zero, one = heads[group - 1 : group, :], heads[1 + group : 2 + group, :]
        ends.append(
            (
                (tap[0] * zero + tap[1] * newer + tap[2] * older).astype(jnp.bfloat16),
                (tap[0] * one + tap[1] * zero + tap[2] * newer).astype(jnp.bfloat16),
            )
        )
    first, second = [gate(k, v).astype(jnp.float32) for k, v in zip(*ends)]
    lane = lax.broadcasted_iota(jnp.int32, (N1, N2), 1)
    row = lax.broadcasted_iota(jnp.int32, (N1, N2), 0)
    for start in range(0, channels, N1):
        cols = slice(start, start + N1)
        to = slice(start // per_dev, (start + N1) // per_dev)
        spread = jnp.where(row == 0, first[:, cols], second[:, cols])
        value = started[cols, :N2].astype(jnp.float32)
        mended = jnp.where(lane < 2, spread.T, value).astype(jnp.bfloat16)
        edge[to, :, :] = mended.reshape(N1 // per_dev, per_dev, N2)
    copies.append(pltpu.make_async_copy(edge, send.at[:, :per_dev, :N2], arrived.at[2]))
    copies[2].start()
    for copy in copies:
        copy.wait()


def query_kernel(projected, taps, rims, query, held, arrived):
    channels, _ = held.shape
    copy = pltpu.make_async_copy(projected.at[0], held, arrived)
    copy.start()
    copy.wait()
    for first in range(0, channels, N1):
        cols = slice(first, first + N1)
        tap = tap_columns(taps, cols)[0]
        rims_t = jnp.concatenate(
            [rims[:, cols].astype(jnp.float32), jnp.zeros((8, N1), jnp.float32)], axis=0
        ).T
        for rows in strips(N1):
            place = slice(first + rows.start, first + rows.stop)
            query[place, :N2], query[place, N2:] = short_feature(
                held[place, :N2],
                held[place, N2:],
                [column[rows] for column in tap],
                rims_t[rows, 0:1],
                rims_t[rows, 3:4],
            )


def product_kernel(query, returned, turned):
    product = query[...].astype(jnp.float32) * returned[...].astype(jnp.float32)
    turned[...] = product.T.astype(jnp.bfloat16)


def own_matmul_kernel(mine, w_out, total, rest, held, arrived):
    me = lax.axis_index("mp")
    quarter = mine.shape[1]
    copies = []
    for flip in range(4):
        rows = pl.ds(pl.multiple_of((me ^ flip) * quarter, quarter), quarter)
        target = rest.at[pl.ds((flip - 1) * quarter, quarter), :] if flip else held
        copy = pltpu.make_async_copy(w_out.at[rows, :], target, arrived.at[flip])
        copy.start()
        copies.append(copy)
    copies[0].wait()
    total[...] = dot(mine[...], held[...])
    for copy in copies[1:]:
        copy.wait()


def last_matmul_kernel(total, value, rest, mixed, held, arrived):
    tokens, out_len = held.shape
    quarter = value.shape[1]
    step = out_len // 4
    copies = []
    for place in range(4):
        cols = slice(place * step, (place + 1) * step)
        held[:, cols] = (total[:, cols] + dot(value[...], rest[2 * quarter :, cols])).astype(
            jnp.bfloat16
        )
        copy = pltpu.make_async_copy(held.at[:, cols], mixed.at[:, cols], arrived.at[place])
        copy.start()
        copies.append(copy)
    for copy in copies:
        copy.wait()


def cost(flops, moved):
    return pl.CostEstimate(flops=flops, bytes_accessed=moved, transcendentals=0)


def whole():
    return pl.BlockSpec(memory_space=pltpu.VMEM)


def in_hbm(value):
    return pltpu.with_memory_space_constraint(value, pltpu.HBM)


PARAMS = pltpu.CompilerParams(vmem_limit_bytes=32 * 2**20)


def per_device(projected, short_taps, long_filter, skip_gain, w_out):
    tok_len = projected.shape[2]
    quarter = projected.shape[1]
    seq_parts = lax.axis_size("seq")
    per_dev = quarter // seq_parts
    chunk = (seq_parts, per_dev, tok_len)
    stage1, turns, forward2, inverse2, inverse1 = [jnp.asarray(table) for table in dft_tables()]
    projected = in_hbm(projected)
    anywhere = pl.BlockSpec(memory_space=pl.ANY)

    def transposed(value):
        return lax.all_to_all(value, "seq", split_axis=0, concat_axis=0, tiled=True)

    tails, pair, filter_here, taps = pl.pallas_call(
        rim_kernel,
        out_shape=[
            jax.ShapeDtypeStruct((8, quarter), jnp.bfloat16),
            jax.ShapeDtypeStruct((2, quarter, tok_len), jnp.bfloat16),
            jax.ShapeDtypeStruct((quarter, tok_len), jnp.bfloat16),
            jax.ShapeDtypeStruct(short_taps.shape, jnp.float32),
        ],
        in_specs=[anywhere] * 3,
        out_specs=[whole()] * 4,
        scratch_shapes=[
            pltpu.VMEM((3, quarter, N2), jnp.bfloat16),
            pltpu.SemaphoreType.DMA((4,)),
        ],
        compiler_params=PARAMS,
        cost_estimate=cost(1000, 1000),
    )(projected, in_hbm(long_filter), in_hbm(short_taps))
    rims = lax.ppermute(tails, "seq", [(s, s + 1) for s in range(seq_parts - 1)])
    started, heads = pl.pallas_call(
        gate_kernel,
        out_shape=[
            jax.ShapeDtypeStruct((quarter, tok_len), jnp.bfloat16),
            jax.ShapeDtypeStruct((8, quarter), jnp.float32),
        ],
        in_specs=[whole()] * 2,
        out_specs=[whole()] * 2,
        compiler_params=PARAMS,
        cost_estimate=cost(1000, 1000),
    )(pair, taps)
    send = pl.pallas_call(
        mend_kernel,
        out_shape=jax.ShapeDtypeStruct((seq_parts, 2 * per_dev, tok_len), jnp.bfloat16),
        in_specs=[whole()] * 5,
        out_specs=anywhere,
        scratch_shapes=[
            pltpu.VMEM((seq_parts, per_dev, N2), jnp.bfloat16),
            pltpu.SemaphoreType.DMA((3,)),
        ],
        compiler_params=PARAMS,
        cost_estimate=cost(1000, 1000),
    )(started, taps, rims, heads, filter_here)
    received = transposed(send)
    query = pl.pallas_call(
        query_kernel,
        out_shape=jax.ShapeDtypeStruct((quarter, tok_len), jnp.bfloat16),
        in_specs=[anywhere, whole(), whole()],
        out_specs=whole(),
        scratch_shapes=[pltpu.VMEM((quarter, tok_len), jnp.bfloat16), pltpu.SemaphoreType.DMA],
        compiler_params=PARAMS,
        cost_estimate=cost(5_000_000, 1_000_000),
    )(projected, taps, rims)
    received, query = lax.optimization_barrier((received, query))

    own_skip = lax.dynamic_slice_in_dim(skip_gain, lax.axis_index("seq") * per_dev, per_dev, 0)
    own_skip = jnp.broadcast_to(own_skip[:, None], (per_dev, N2))
    response = pl.pallas_call(
        conv_kernel,
        out_shape=jax.ShapeDtypeStruct(chunk, jnp.bfloat16),
        in_specs=[whole()] * 7,
        out_specs=whole(),
        scratch_shapes=[
            pltpu.VMEM((seq_parts * (rows + GAP), N2), jnp.float32)
            for rows in (2 * per_dev, 2 * per_dev, per_dev, per_dev)
        ]
        + [pltpu.VMEM((per_dev * N1, 2 * N2), jnp.float32) for _ in range(2)],
        compiler_params=PARAMS,
        cost_estimate=cost(6_000_000_000, 4_000_000),
    )(received, own_skip, stage1, turns, forward2, inverse2, inverse1)
    returned = transposed(response)

    product = pl.pallas_call(
        product_kernel,
        out_shape=jax.ShapeDtypeStruct((tok_len, quarter), jnp.bfloat16),
        in_specs=[whole()] * 2,
        out_specs=whole(),
        compiler_params=PARAMS,
        cost_estimate=cost(1_000_000, 1_500_000),
    )(query, returned.reshape(quarter, tok_len))

    me = lax.axis_index("mp")
    to_far = [(m, m ^ 2) for m in range(4)]
    to_near = [(m, m ^ 1) for m in range(4)]

    far = lax.ppermute(product, "mp", to_far)
    near = lax.ppermute(product, "mp", to_near)
    out_len = w_out.shape[1]
    total, rest = pl.pallas_call(
        own_matmul_kernel,
        out_shape=[
            jax.ShapeDtypeStruct((tok_len, out_len), jnp.float32),
            jax.ShapeDtypeStruct((3 * quarter, out_len), jnp.bfloat16),
        ],
        in_specs=[whole(), anywhere],
        out_specs=[whole()] * 2,
        scratch_shapes=[pltpu.VMEM((quarter, out_len), jnp.bfloat16), pltpu.SemaphoreType.DMA((4,))],
        compiler_params=PARAMS,
        cost_estimate=cost(1000, 1000),
    )(product, in_hbm(w_out))
    total, rest, far = lax.optimization_barrier((total, rest, far))
    last = lax.ppermute(far, "mp", to_near)
    total = total + dot(far, rest[quarter : 2 * quarter])
    total = total + dot(near, rest[:quarter])
    return pl.pallas_call(
        last_matmul_kernel,
        out_shape=jax.ShapeDtypeStruct((tok_len, out_len), jnp.bfloat16),
        in_specs=[whole()] * 3,
        out_specs=anywhere,
        scratch_shapes=[
            pltpu.VMEM((tok_len, out_len), jnp.bfloat16),
            pltpu.SemaphoreType.DMA((4,)),
        ],
        compiler_params=PARAMS,
        cost_estimate=cost(500_000_000, 4_000_000),
    )(total, last, rest)


def solution(mesh):
    return jax.shard_map(
        per_device,
        mesh=mesh,
        in_specs=(
            P(None, "mp", "seq"),
            P(None, None, "mp"),
            P("mp", "seq"),
            P("mp"),
            P(None, "mp"),
        ),
        out_specs=P("seq", "mp"),
        check_vma=False,
    )
```

```python
import jax
import jax.numpy as jnp
import ml_dtypes
import numpy as np
from jax import lax
from jax.experimental import pallas as pl
from jax.experimental.pallas import tpu as pltpu
from jax.sharding import PartitionSpec as P

N1 = 128
N2 = 128
GROUP = 16
GAP = 8
STRIP = 64


def split(table):
    high = table.astype(ml_dtypes.bfloat16)
    low = (table - high.astype(np.float64)).astype(ml_dtypes.bfloat16)
    return high, low


def dft_tables():
    order = np.concatenate([np.arange(0, N1, 2), np.arange(1, N1, 2)])
    k1 = np.arange(N1)
    first = 2.0 * np.pi * np.outer(k1 + 0.25, order) / N1
    stage1 = np.concatenate(split(np.concatenate([np.cos(first), -np.sin(first)], axis=0)), axis=1)
    turn = 2.0 * np.pi * np.outer(k1 + 0.25, np.arange(N2)) / (N1 * N2)
    turns = np.stack([np.cos(turn), np.sin(turn)]).astype(np.float32)
    second = 2.0 * np.pi * np.outer(np.arange(N2), np.arange(N2)) / N2
    cos, sin = np.cos(second), np.sin(second)
    high, low = split(np.block([[cos, -sin], [sin, cos]]))
    forward2 = np.concatenate([high, high, low], axis=0)
    high, low = split(np.block([[cos, sin], [-sin, cos]]))
    inverse2 = np.concatenate([high, low], axis=0)
    last = np.concatenate([np.cos(first.T), -np.sin(first.T)], axis=1) / (N1 * N2)
    inverse1 = np.concatenate(split(last), axis=0)
    return stage1, turns, forward2, inverse2, inverse1


def dot(a, b):
    return jnp.dot(a, b, preferred_element_type=jnp.float32)


def halves(value):
    high = value.astype(jnp.bfloat16)
    low = (value - high.astype(jnp.float32)).astype(jnp.bfloat16)
    return high, low


def split_dot(wide, table):
    middle = wide.shape[0] // 2
    return jnp.concatenate([dot(wide[:middle], table), dot(wide[middle:], table)], axis=0)


def wide_dot(value, table):
    high, low = halves(value)
    return split_dot(jnp.concatenate([high, low, high], axis=1), table)


def load_tile(flat, row, parts, stride):
    return jnp.concatenate([half[pl.ds(row, parts, stride=stride), :] for half in flat], axis=0)


def spectra_of(tiles, stage1, turns, forward2):
    cos, sin = turns[0], turns[1]
    turned = []
    for first in range(0, len(tiles), 2):
        pair = jnp.concatenate(tiles[first : first + 2], axis=1).astype(jnp.bfloat16)
        both = dot(stage1[...], jnp.concatenate([pair, pair], axis=0))
        for place in range(2):
            re = both[:N1, place * N2 : (place + 1) * N2]
            im = both[N1:, place * N2 : (place + 1) * N2]
            turned.append(jnp.concatenate([re * cos + im * sin, im * cos - re * sin], axis=1))
    return wide_dot(jnp.concatenate(turned, axis=0), forward2[...])


def conv_kernel(
    received, skip, stage1, turns, forward2, inverse2, inverse1, response,
    even, odd, out_even, out_odd, product, spectrum,
):
    parts, rows, _ = received.shape
    per_dev = rows // 2
    flat, out_flat = (even, odd), (out_even, out_odd)
    lanes = [slice(half * N2, (half + 1) * N2) for half in range(2)]
    in_step, out_step = rows + GAP, per_dev + GAP
    for half in range(2):
        for part in range(parts):
            flat[half][part * in_step : part * in_step + rows, :] = received[
                part, :, lanes[half]
            ].astype(jnp.float32)
    for start, spectra in ((per_dev, spectrum), (0, product)):
        for first in range(0, per_dev, GROUP):
            tiles = [load_tile(flat, start + first + c, parts, in_step) for c in range(GROUP)]
            spectra[first * N1 : (first + GROUP) * N1, :] = spectra_of(tiles, stage1, turns, forward2)
    cos, sin = turns[0], turns[1]
    for first in range(0, per_dev, GROUP):
        span = slice(first * N1, (first + GROUP) * N1)
        sig_re, sig_im = product[span, :N2], product[span, N2:]
        ker_re, ker_im = spectrum[span, :N2], spectrum[span, N2:]
        multiplied = jnp.concatenate(
            [sig_re * ker_re - sig_im * ker_im, sig_re * ker_im + sig_im * ker_re], axis=1
        )
        held = multiplied.astype(jnp.bfloat16)
        back = split_dot(jnp.concatenate([held, held], axis=1), inverse2[...])
        for c in range(0, GROUP, 2):
            turned = []
            for place in (c, c + 1):
                re = back[place * N1 : (place + 1) * N1, :N2]
                im = back[place * N1 : (place + 1) * N1, N2:]
                turned.append(jnp.concatenate([re * cos - im * sin, re * sin + im * cos], axis=0))
            both = dot(inverse1[...], jnp.concatenate(turned, axis=1).astype(jnp.bfloat16))
            restored = both[:N1] + both[N1:]
            for place in range(2):
                channel = first + c + place
                out = restored[:, place * N2 : (place + 1) * N2]
                for half in range(2):
                    out_flat[half][pl.ds(channel, parts, stride=out_step), :] = out[
                        half * parts : (half + 1) * parts
                    ]
    for half in range(2):
        for part in range(parts):
            direct = skip[...] * received[part, :per_dev, lanes[half]].astype(jnp.float32)
            convolved = out_flat[half][part * out_step : part * out_step + per_dev, :]
            response[part, :, lanes[half]] = (convolved + direct).astype(jnp.bfloat16)


def tap_columns(taps, cols):
    rows = [taps[group] for group in range(3)] + [jnp.zeros((7, taps.shape[2]), jnp.float32)]
    columns = jnp.concatenate([row[:, cols] for row in rows], axis=0).T
    return [[columns[:, 3 * g + p : 3 * g + p + 1] for p in range(3)] for g in range(3)]


def weigh(tap, value, back1, back2):
    return (tap[0] * value + tap[1] * back1 + tap[2] * back2).astype(jnp.bfloat16)


def short_feature(left, right, tap, older, newer):
    left, right = left.astype(jnp.float32), right.astype(jnp.float32)
    lane = lax.broadcasted_iota(jnp.int32, left.shape, 1)
    left1, left2 = pltpu.roll(left, 1, 1), pltpu.roll(left, 2, 1)
    right1 = jnp.where(lane < 1, left1, pltpu.roll(right, 1, 1))
    right2 = jnp.where(lane < 2, left2, pltpu.roll(right, 2, 1))
    left1 = jnp.where(lane < 1, newer, left1)
    left2 = jnp.where(lane < 1, older, jnp.where(lane < 2, newer, left2))
    return weigh(tap, left, left1, left2), weigh(tap, right, right1, right2)


def gate(k, v):
    return (k.astype(jnp.float32) * v.astype(jnp.float32)).astype(jnp.bfloat16)


def strips(channels):
    return [slice(first, first + STRIP) for first in range(0, channels, STRIP)]


def edge_rows(pick, tiles):
    return [
        lax.dot_general(pick, tile, (((1,), (1,)), ((), ())), preferred_element_type=jnp.float32)
        for tile in tiles
    ]


def picker(lanes):
    row = lax.broadcasted_iota(jnp.int32, (16, N2), 0)
    lane = lax.broadcasted_iota(jnp.int32, (16, N2), 1)
    hit = jnp.zeros((16, N2), jnp.bool_)
    for place, wanted in enumerate(lanes):
        hit = hit | ((row == place) & (lane == wanted))
    return jnp.where(hit, 1.0, 0.0).astype(jnp.bfloat16)


def rim_kernel(projected, long_filter, short_taps, tails, pair, filter_out, taps, edge, arrived):
    groups, channels, _ = edge.shape
    moves = (
        (projected.at[:, :, N2:], edge),
        (projected.at[1:], pair),
        (long_filter, filter_out),
        (short_taps, taps),
    )
    copies = [
        pltpu.make_async_copy(source, target, arrived.at[place])
        for place, (source, target) in enumerate(moves)
    ]
    for copy in copies:
        copy.start()
    copies[0].wait()
    rows = edge_rows(picker((N2 - 2, N2 - 1)), [edge[group] for group in range(groups)])
    picked = [t[place : place + 1] for place in range(2) for t in rows]
    picked.append(jnp.zeros((2, channels), jnp.float32))
    tails[...] = jnp.concatenate(picked, axis=0).astype(jnp.bfloat16)
    for copy in copies[1:]:
        copy.wait()


def gate_kernel(pair, taps, gated, heads):
    _, channels, _ = pair.shape
    for first in range(0, channels, N1):
        columns = tap_columns(taps, slice(first, first + N1))
        for rows in strips(N1):
            place = slice(first + rows.start, first + rows.stop)
            k, v = [
                short_feature(
                    pair[group - 1, place, :N2],
                    pair[group - 1, place, N2:],
                    [column[rows] for column in columns[group]],
                    0.0,
                    0.0,
                )
                for group in (1, 2)
            ]
            gated[place, :N2] = gate(k[0], v[0])
            gated[place, N2:] = gate(k[1], v[1])
    rows = edge_rows(picker((0, 1)), [pair[group, :, :N2] for group in range(2)])
    picked = [t[place : place + 1] for place in range(2) for t in rows]
    picked.append(jnp.zeros((4, channels), jnp.float32))
    heads[...] = jnp.concatenate(picked, axis=0)


def mend_kernel(started, taps, rims, heads, long_filter, send, edge, arrived):
    dests, per_dev, _ = edge.shape
    channels = dests * per_dev
    copies = [
        pltpu.make_async_copy(
            started.reshape(dests, per_dev, 2 * N2).at[:, :, N2:],
            send.at[:, :per_dev, N2:],
            arrived.at[0],
        ),
        pltpu.make_async_copy(
            long_filter.reshape(dests, per_dev, 2 * N2), send.at[:, per_dev:, :], arrived.at[1]
        ),
    ]
    for copy in copies:
        copy.start()
    ends = []
    for group in (1, 2):
        tap = [taps[group, place : place + 1, :] for place in range(3)]
        older = rims[group : group + 1, :].astype(jnp.float32)
        newer = rims[3 + group : 4 + group, :].astype(jnp.float32)
        zero, one = heads[group - 1 : group, :], heads[1 + group : 2 + group, :]
        ends.append(
            (
                (tap[0] * zero + tap[1] * newer + tap[2] * older).astype(jnp.bfloat16),
                (tap[0] * one + tap[1] * zero + tap[2] * newer).astype(jnp.bfloat16),
            )
        )
    first, second = [gate(k, v).astype(jnp.float32) for k, v in zip(*ends)]
    lane = lax.broadcasted_iota(jnp.int32, (N1, N2), 1)
    row = lax.broadcasted_iota(jnp.int32, (N1, N2), 0)
    for start in range(0, channels, N1):
        cols = slice(start, start + N1)
        to = slice(start // per_dev, (start + N1) // per_dev)
        spread = jnp.where(row == 0, first[:, cols], second[:, cols])
        value = started[cols, :N2].astype(jnp.float32)
        mended = jnp.where(lane < 2, spread.T, value).astype(jnp.bfloat16)
        edge[to, :, :] = mended.reshape(N1 // per_dev, per_dev, N2)
    copies.append(pltpu.make_async_copy(edge, send.at[:, :per_dev, :N2], arrived.at[2]))
    copies[2].start()
    for copy in copies:
        copy.wait()


def query_kernel(projected, taps, rims, query, held, arrived):
    channels, _ = held.shape
    copy = pltpu.make_async_copy(projected.at[0], held, arrived)
    copy.start()
    copy.wait()
    for first in range(0, channels, N1):
        cols = slice(first, first + N1)
        tap = tap_columns(taps, cols)[0]
        rims_t = jnp.concatenate(
            [rims[:, cols].astype(jnp.float32), jnp.zeros((8, N1), jnp.float32)], axis=0
        ).T
        for rows in strips(N1):
            place = slice(first + rows.start, first + rows.stop)
            query[place, :N2], query[place, N2:] = short_feature(
                held[place, :N2],
                held[place, N2:],
                [column[rows] for column in tap],
                rims_t[rows, 0:1],
                rims_t[rows, 3:4],
            )


def product_kernel(query, returned, turned):
    product = query[...].astype(jnp.float32) * returned[...].astype(jnp.float32)
    turned[...] = product.T.astype(jnp.bfloat16)


def own_matmul_kernel(mine, w_out, total, rest, held, arrived):
    me = lax.axis_index("mp")
    quarter = mine.shape[1]
    copies = []
    for flip in range(4):
        rows = pl.ds(pl.multiple_of((me ^ flip) * quarter, quarter), quarter)
        target = rest.at[pl.ds((flip - 1) * quarter, quarter), :] if flip else held
        copy = pltpu.make_async_copy(w_out.at[rows, :], target, arrived.at[flip])
        copy.start()
        copies.append(copy)
    copies[0].wait()
    total[...] = dot(mine[...], held[...])
    for copy in copies[1:]:
        copy.wait()


def last_matmul_kernel(total, value, rest, mixed, held, arrived):
    tokens, out_len = held.shape
    quarter = value.shape[1]
    step = out_len // 4
    copies = []
    for place in range(4):
        cols = slice(place * step, (place + 1) * step)
        held[:, cols] = (total[:, cols] + dot(value[...], rest[2 * quarter :, cols])).astype(
            jnp.bfloat16
        )
        copy = pltpu.make_async_copy(held.at[:, cols], mixed.at[:, cols], arrived.at[place])
        copy.start()
        copies.append(copy)
    for copy in copies:
        copy.wait()


def cost(flops, moved):
    return pl.CostEstimate(flops=flops, bytes_accessed=moved, transcendentals=0)


def whole():
    return pl.BlockSpec(memory_space=pltpu.VMEM)


def in_hbm(value):
    return pltpu.with_memory_space_constraint(value, pltpu.HBM)


PARAMS = pltpu.CompilerParams(vmem_limit_bytes=32 * 2**20)


def per_device(projected, short_taps, long_filter, skip_gain, w_out):
    tok_len = projected.shape[2]
    quarter = projected.shape[1]
    seq_parts = lax.axis_size("seq")
    per_dev = quarter // seq_parts
    chunk = (seq_parts, per_dev, tok_len)
    stage1, turns, forward2, inverse2, inverse1 = [jnp.asarray(table) for table in dft_tables()]
    projected = in_hbm(projected)
    anywhere = pl.BlockSpec(memory_space=pl.ANY)

    def transposed(value):
        return lax.all_to_all(value, "seq", split_axis=0, concat_axis=0, tiled=True)

    tails, pair, filter_here, taps = pl.pallas_call(
        rim_kernel,
        out_shape=[
            jax.ShapeDtypeStruct((8, quarter), jnp.bfloat16),
            jax.ShapeDtypeStruct((2, quarter, tok_len), jnp.bfloat16),
            jax.ShapeDtypeStruct((quarter, tok_len), jnp.bfloat16),
            jax.ShapeDtypeStruct(short_taps.shape, jnp.float32),
        ],
        in_specs=[anywhere] * 3,
        out_specs=[whole()] * 4,
        scratch_shapes=[
            pltpu.VMEM((3, quarter, N2), jnp.bfloat16),
            pltpu.SemaphoreType.DMA((4,)),
        ],
        compiler_params=PARAMS,
        cost_estimate=cost(1000, 1000),
    )(projected, in_hbm(long_filter), in_hbm(short_taps))
    rims = lax.ppermute(tails, "seq", [(s, s + 1) for s in range(seq_parts - 1)])
    started, heads = pl.pallas_call(
        gate_kernel,
        out_shape=[
            jax.ShapeDtypeStruct((quarter, tok_len), jnp.bfloat16),
            jax.ShapeDtypeStruct((8, quarter), jnp.float32),
        ],
        in_specs=[whole()] * 2,
        out_specs=[whole()] * 2,
        compiler_params=PARAMS,
        cost_estimate=cost(1000, 1000),
    )(pair, taps)
    send = pl.pallas_call(
        mend_kernel,
        out_shape=jax.ShapeDtypeStruct((seq_parts, 2 * per_dev, tok_len), jnp.bfloat16),
        in_specs=[whole()] * 5,
        out_specs=anywhere,
        scratch_shapes=[
            pltpu.VMEM((seq_parts, per_dev, N2), jnp.bfloat16),
            pltpu.SemaphoreType.DMA((3,)),
        ],
        compiler_params=PARAMS,
        cost_estimate=cost(1000, 1000),
    )(started, taps, rims, heads, filter_here)
    received = transposed(send)
    query = pl.pallas_call(
        query_kernel,
        out_shape=jax.ShapeDtypeStruct((quarter, tok_len), jnp.bfloat16),
        in_specs=[anywhere, whole(), whole()],
        out_specs=whole(),
        scratch_shapes=[pltpu.VMEM((quarter, tok_len), jnp.bfloat16), pltpu.SemaphoreType.DMA],
        compiler_params=PARAMS,
        cost_estimate=cost(5_000_000, 1_000_000),
    )(projected, taps, rims)
    received, query = lax.optimization_barrier((received, query))

    own_skip = lax.dynamic_slice_in_dim(skip_gain, lax.axis_index("seq") * per_dev, per_dev, 0)
    own_skip = jnp.broadcast_to(own_skip[:, None], (per_dev, N2))
    response = pl.pallas_call(
        conv_kernel,
        out_shape=jax.ShapeDtypeStruct(chunk, jnp.bfloat16),
        in_specs=[whole()] * 7,
        out_specs=whole(),
        scratch_shapes=[
            pltpu.VMEM((seq_parts * (rows + GAP), N2), jnp.float32)
            for rows in (2 * per_dev, 2 * per_dev, per_dev, per_dev)
        ]
        + [pltpu.VMEM((per_dev * N1, 2 * N2), jnp.float32) for _ in range(2)],
        compiler_params=PARAMS,
        cost_estimate=cost(6_000_000_000, 4_000_000),
    )(received, own_skip, stage1, turns, forward2, inverse2, inverse1)
    returned = transposed(response)

    product = pl.pallas_call(
        product_kernel,
        out_shape=jax.ShapeDtypeStruct((tok_len, quarter), jnp.bfloat16),
        in_specs=[whole()] * 2,
        out_specs=whole(),
        compiler_params=PARAMS,
        cost_estimate=cost(1_000_000, 1_500_000),
    )(query, returned.reshape(quarter, tok_len))

    me = lax.axis_index("mp")
    to_far = [(m, m ^ 2) for m in range(4)]
    to_near = [(m, m ^ 1) for m in range(4)]

    far = lax.ppermute(product, "mp", to_far)
    near = lax.ppermute(product, "mp", to_near)
    out_len = w_out.shape[1]
    total, rest = pl.pallas_call(
        own_matmul_kernel,
        out_shape=[
            jax.ShapeDtypeStruct((tok_len, out_len), jnp.float32),
            jax.ShapeDtypeStruct((3 * quarter, out_len), jnp.bfloat16),
        ],
        in_specs=[whole(), anywhere],
        out_specs=[whole()] * 2,
        scratch_shapes=[pltpu.VMEM((quarter, out_len), jnp.bfloat16), pltpu.SemaphoreType.DMA((4,))],
        compiler_params=PARAMS,
        cost_estimate=cost(1000, 1000),
    )(product, in_hbm(w_out))
    total, rest, far = lax.optimization_barrier((total, rest, far))
    last = lax.ppermute(far, "mp", to_near)
    total = total + dot(far, rest[quarter : 2 * quarter])
    total = total + dot(near, rest[:quarter])
    return pl.pallas_call(
        last_matmul_kernel,
        out_shape=jax.ShapeDtypeStruct((tok_len, out_len), jnp.bfloat16),
        in_specs=[whole()] * 3,
        out_specs=anywhere,
        scratch_shapes=[
            pltpu.VMEM((tok_len, out_len), jnp.bfloat16),
            pltpu.SemaphoreType.DMA((4,)),
        ],
        compiler_params=PARAMS,
        cost_estimate=cost(500_000_000, 4_000_000),
    )(total, last, rest)


def solution(mesh):
    return jax.shard_map(
        per_device,
        mesh=mesh,
        in_specs=(
            P(None, "mp", "seq"),
            P(None, None, "mp"),
            P("mp", "seq"),
            P("mp"),
            P(None, "mp"),
        ),
        out_specs=P("seq", "mp"),
        check_vma=False,
    )
```

```python
import jax
import jax.numpy as jnp
import ml_dtypes
import numpy as np
from jax import lax
from jax.experimental import pallas as pl
from jax.experimental.pallas import tpu as pltpu
from jax.sharding import PartitionSpec as P

N1 = 128
N2 = 128
GROUP = 16
GAP = 8
STRIP = 64


def split(table):
    high = table.astype(ml_dtypes.bfloat16)
    low = (table - high.astype(np.float64)).astype(ml_dtypes.bfloat16)
    return high, low


def dft_tables():
    order = np.concatenate([np.arange(0, N1, 2), np.arange(1, N1, 2)])
    k1 = np.arange(N1)
    first = 2.0 * np.pi * np.outer(k1 + 0.25, order) / N1
    stage1 = np.concatenate(split(np.concatenate([np.cos(first), -np.sin(first)], axis=0)), axis=1)
    turn = 2.0 * np.pi * np.outer(k1 + 0.25, np.arange(N2)) / (N1 * N2)
    turns = np.stack([np.cos(turn), np.sin(turn)]).astype(np.float32)
    second = 2.0 * np.pi * np.outer(np.arange(N2), np.arange(N2)) / N2
    cos, sin = np.cos(second), np.sin(second)
    high, low = split(np.block([[cos, -sin], [sin, cos]]))
    forward2 = np.concatenate([high, high, low], axis=0)
    high, low = split(np.block([[cos, sin], [-sin, cos]]))
    inverse2 = np.concatenate([high, high, low], axis=0)
    last = np.concatenate([np.cos(first.T), -np.sin(first.T)], axis=1) / (N1 * N2)
    inverse1 = np.concatenate(split(last), axis=0)
    return stage1, turns, forward2, inverse2, inverse1


def dot(a, b):
    return jnp.dot(a, b, preferred_element_type=jnp.float32)


def halves(value):
    high = value.astype(jnp.bfloat16)
    low = (value - high.astype(jnp.float32)).astype(jnp.bfloat16)
    return high, low


def wide_dot(value, table):
    high, low = halves(value)
    wide = jnp.concatenate([high, low, high], axis=1)
    middle = wide.shape[0] // 2
    return jnp.concatenate([dot(wide[:middle], table), dot(wide[middle:], table)], axis=0)


def load_tile(flat, row, parts, stride):
    return jnp.concatenate([half[pl.ds(row, parts, stride=stride), :] for half in flat], axis=0)


def spectra_of(tiles, stage1, turns, forward2):
    cos, sin = turns[0], turns[1]
    turned = []
    for first in range(0, len(tiles), 2):
        pair = jnp.concatenate(tiles[first : first + 2], axis=1).astype(jnp.bfloat16)
        both = dot(stage1[...], jnp.concatenate([pair, pair], axis=0))
        for place in range(2):
            re = both[:N1, place * N2 : (place + 1) * N2]
            im = both[N1:, place * N2 : (place + 1) * N2]
            turned.append(jnp.concatenate([re * cos + im * sin, im * cos - re * sin], axis=1))
    return wide_dot(jnp.concatenate(turned, axis=0), forward2[...])


def conv_kernel(
    received, skip, stage1, turns, forward2, inverse2, inverse1, response,
    even, odd, out_even, out_odd, product, spectrum,
):
    parts, rows, _ = received.shape
    per_dev = rows // 2
    flat, out_flat = (even, odd), (out_even, out_odd)
    lanes = [slice(half * N2, (half + 1) * N2) for half in range(2)]
    in_step, out_step = rows + GAP, per_dev + GAP
    for half in range(2):
        for part in range(parts):
            flat[half][part * in_step : part * in_step + rows, :] = received[
                part, :, lanes[half]
            ].astype(jnp.float32)
    for start, spectra in ((per_dev, spectrum), (0, product)):
        for first in range(0, per_dev, GROUP):
            tiles = [load_tile(flat, start + first + c, parts, in_step) for c in range(GROUP)]
            spectra[first * N1 : (first + GROUP) * N1, :] = spectra_of(tiles, stage1, turns, forward2)
    cos, sin = turns[0], turns[1]
    for first in range(0, per_dev, GROUP):
        span = slice(first * N1, (first + GROUP) * N1)
        sig_re, sig_im = product[span, :N2], product[span, N2:]
        ker_re, ker_im = spectrum[span, :N2], spectrum[span, N2:]
        multiplied = jnp.concatenate(
            [sig_re * ker_re - sig_im * ker_im, sig_re * ker_im + sig_im * ker_re], axis=1
        )
        back = wide_dot(multiplied, inverse2[...])
        for c in range(0, GROUP, 2):
            turned = []
            for place in (c, c + 1):
                re = back[place * N1 : (place + 1) * N1, :N2]
                im = back[place * N1 : (place + 1) * N1, N2:]
                turned.append(jnp.concatenate([re * cos - im * sin, re * sin + im * cos], axis=0))
            high, low = halves(jnp.concatenate(turned, axis=1))
            most = dot(inverse1[...], high)
            restored = most[:N1] + (most[N1:] + dot(inverse1[:N1, :], low))
            for place in range(2):
                channel = first + c + place
                out = restored[:, place * N2 : (place + 1) * N2]
                for half in range(2):
                    out_flat[half][pl.ds(channel, parts, stride=out_step), :] = out[
                        half * parts : (half + 1) * parts
                    ]
    for half in range(2):
        for part in range(parts):
            direct = skip[...] * received[part, :per_dev, lanes[half]].astype(jnp.float32)
            convolved = out_flat[half][part * out_step : part * out_step + per_dev, :]
            response[part, :, lanes[half]] = (convolved + direct).astype(jnp.bfloat16)


def tap_columns(taps, cols):
    rows = [taps[group] for group in range(3)] + [jnp.zeros((7, taps.shape[2]), jnp.float32)]
    columns = jnp.concatenate([row[:, cols] for row in rows], axis=0).T
    return [[columns[:, 3 * g + p : 3 * g + p + 1] for p in range(3)] for g in range(3)]


def weigh(tap, value, back1, back2):
    return (tap[0] * value + tap[1] * back1 + tap[2] * back2).astype(jnp.bfloat16)


def short_feature(left, right, tap, older, newer):
    left, right = left.astype(jnp.float32), right.astype(jnp.float32)
    lane = lax.broadcasted_iota(jnp.int32, left.shape, 1)
    left1, left2 = pltpu.roll(left, 1, 1), pltpu.roll(left, 2, 1)
    right1 = jnp.where(lane < 1, left1, pltpu.roll(right, 1, 1))
    right2 = jnp.where(lane < 2, left2, pltpu.roll(right, 2, 1))
    left1 = jnp.where(lane < 1, newer, left1)
    left2 = jnp.where(lane < 1, older, jnp.where(lane < 2, newer, left2))
    return weigh(tap, left, left1, left2), weigh(tap, right, right1, right2)


def gate(k, v):
    return (k.astype(jnp.float32) * v.astype(jnp.float32)).astype(jnp.bfloat16)


def strips(channels):
    return [slice(first, first + STRIP) for first in range(0, channels, STRIP)]


def edge_rows(pick, tiles):
    return [
        lax.dot_general(pick, tile, (((1,), (1,)), ((), ())), preferred_element_type=jnp.float32)
        for tile in tiles
    ]


def picker(lanes):
    row = lax.broadcasted_iota(jnp.int32, (16, N2), 0)
    lane = lax.broadcasted_iota(jnp.int32, (16, N2), 1)
    hit = jnp.zeros((16, N2), jnp.bool_)
    for place, wanted in enumerate(lanes):
        hit = hit | ((row == place) & (lane == wanted))
    return jnp.where(hit, 1.0, 0.0).astype(jnp.bfloat16)


def rim_kernel(projected, short_taps, tails, pair, taps, edge, arrived):
    groups, channels, _ = edge.shape
    moves = (
        (projected.at[:, :, N2:], edge),
        (projected.at[1:], pair),
        (short_taps, taps),
    )
    copies = [
        pltpu.make_async_copy(source, target, arrived.at[place])
        for place, (source, target) in enumerate(moves)
    ]
    for copy in copies:
        copy.start()
    copies[0].wait()
    rows = edge_rows(picker((N2 - 2, N2 - 1)), [edge[group] for group in range(groups)])
    picked = [t[place : place + 1] for place in range(2) for t in rows]
    picked.append(jnp.zeros((2, channels), jnp.float32))
    tails[...] = jnp.concatenate(picked, axis=0).astype(jnp.bfloat16)
    for copy in copies[1:]:
        copy.wait()


def gate_kernel(pair, taps, long_filter, gated, heads, filter_out, arrived):
    _, channels, _ = pair.shape
    copy = pltpu.make_async_copy(long_filter, filter_out, arrived)
    copy.start()
    for first in range(0, channels, N1):
        columns = tap_columns(taps, slice(first, first + N1))
        for rows in strips(N1):
            place = slice(first + rows.start, first + rows.stop)
            k, v = [
                short_feature(
                    pair[group - 1, place, :N2],
                    pair[group - 1, place, N2:],
                    [column[rows] for column in columns[group]],
                    0.0,
                    0.0,
                )
                for group in (1, 2)
            ]
            gated[place, :N2] = gate(k[0], v[0])
            gated[place, N2:] = gate(k[1], v[1])
    rows = edge_rows(picker((0, 1)), [pair[group, :, :N2] for group in range(2)])
    picked = [t[place : place + 1] for place in range(2) for t in rows]
    picked.append(jnp.zeros((4, channels), jnp.float32))
    heads[...] = jnp.concatenate(picked, axis=0)
    copy.wait()


def mend_kernel(started, taps, rims, heads, long_filter, send, edge, arrived):
    dests, per_dev, _ = edge.shape
    channels = dests * per_dev
    copies = [
        pltpu.make_async_copy(
            started.reshape(dests, per_dev, 2 * N2).at[:, :, N2:],
            send.at[:, :per_dev, N2:],
            arrived.at[0],
        ),
        pltpu.make_async_copy(
            long_filter.reshape(dests, per_dev, 2 * N2), send.at[:, per_dev:, :], arrived.at[1]
        ),
    ]
    for copy in copies:
        copy.start()
    ends = []
    for group in (1, 2):
        tap = [taps[group, place : place + 1, :] for place in range(3)]
        older = rims[group : group + 1, :].astype(jnp.float32)
        newer = rims[3 + group : 4 + group, :].astype(jnp.float32)
        zero, one = heads[group - 1 : group, :], heads[1 + group : 2 + group, :]
        ends.append(
            (
                (tap[0] * zero + tap[1] * newer + tap[2] * older).astype(jnp.bfloat16),
                (tap[0] * one + tap[1] * zero + tap[2] * newer).astype(jnp.bfloat16),
            )
        )
    first, second = [gate(k, v).astype(jnp.float32) for k, v in zip(*ends)]
    lane = lax.broadcasted_iota(jnp.int32, (N1, N2), 1)
    row = lax.broadcasted_iota(jnp.int32, (N1, N2), 0)
    for start in range(0, channels, N1):
        cols = slice(start, start + N1)
        to = slice(start // per_dev, (start + N1) // per_dev)
        spread = jnp.where(row == 0, first[:, cols], second[:, cols])
        value = started[cols, :N2].astype(jnp.float32)
        mended = jnp.where(lane < 2, spread.T, value).astype(jnp.bfloat16)
        edge[to, :, :] = mended.reshape(N1 // per_dev, per_dev, N2)
    copies.append(pltpu.make_async_copy(edge, send.at[:, :per_dev, :N2], arrived.at[2]))
    copies[2].start()
    for copy in copies:
        copy.wait()


def query_kernel(projected, taps, rims, query, held, arrived):
    channels, _ = held.shape
    copy = pltpu.make_async_copy(projected.at[0], held, arrived)
    copy.start()
    copy.wait()
    for first in range(0, channels, N1):
        cols = slice(first, first + N1)
        tap = tap_columns(taps, cols)[0]
        rims_t = jnp.concatenate(
            [rims[:, cols].astype(jnp.float32), jnp.zeros((8, N1), jnp.float32)], axis=0
        ).T
        for rows in strips(N1):
            place = slice(first + rows.start, first + rows.stop)
            query[place, :N2], query[place, N2:] = short_feature(
                held[place, :N2],
                held[place, N2:],
                [column[rows] for column in tap],
                rims_t[rows, 0:1],
                rims_t[rows, 3:4],
            )


def product_kernel(query, returned, turned):
    product = query[...].astype(jnp.float32) * returned[...].astype(jnp.float32)
    turned[...] = product.T.astype(jnp.bfloat16)


def own_matmul_kernel(mine, w_out, total, rest, held, arrived):
    me = lax.axis_index("mp")
    quarter = mine.shape[1]
    copies = []
    for flip in range(4):
        rows = pl.ds(pl.multiple_of((me ^ flip) * quarter, quarter), quarter)
        target = rest.at[pl.ds((flip - 1) * quarter, quarter), :] if flip else held
        copy = pltpu.make_async_copy(w_out.at[rows, :], target, arrived.at[flip])
        copy.start()
        copies.append(copy)
    copies[0].wait()
    total[...] = dot(mine[...], held[...])
    for copy in copies[1:]:
        copy.wait()


def last_matmul_kernel(total, value, rest, mixed, held, arrived):
    tokens, out_len = held.shape
    quarter = value.shape[1]
    step = out_len // 4
    copies = []
    for place in range(4):
        cols = slice(place * step, (place + 1) * step)
        held[:, cols] = (total[:, cols] + dot(value[...], rest[2 * quarter :, cols])).astype(
            jnp.bfloat16
        )
        copy = pltpu.make_async_copy(held.at[:, cols], mixed.at[:, cols], arrived.at[place])
        copy.start()
        copies.append(copy)
    for copy in copies:
        copy.wait()


def cost(flops, moved):
    return pl.CostEstimate(flops=flops, bytes_accessed=moved, transcendentals=0)


def whole():
    return pl.BlockSpec(memory_space=pltpu.VMEM)


def in_hbm(value):
    return pltpu.with_memory_space_constraint(value, pltpu.HBM)


PARAMS = pltpu.CompilerParams(vmem_limit_bytes=32 * 2**20)


def per_device(projected, short_taps, long_filter, skip_gain, w_out):
    tok_len = projected.shape[2]
    quarter = projected.shape[1]
    seq_parts = lax.axis_size("seq")
    per_dev = quarter // seq_parts
    chunk = (seq_parts, per_dev, tok_len)
    stage1, turns, forward2, inverse2, inverse1 = [jnp.asarray(table) for table in dft_tables()]
    projected = in_hbm(projected)
    anywhere = pl.BlockSpec(memory_space=pl.ANY)

    def transposed(value):
        return lax.all_to_all(value, "seq", split_axis=0, concat_axis=0, tiled=True)

    tails, pair, taps = pl.pallas_call(
        rim_kernel,
        out_shape=[
            jax.ShapeDtypeStruct((8, quarter), jnp.bfloat16),
            jax.ShapeDtypeStruct((2, quarter, tok_len), jnp.bfloat16),
            jax.ShapeDtypeStruct(short_taps.shape, jnp.float32),
        ],
        in_specs=[anywhere] * 2,
        out_specs=[whole()] * 3,
        scratch_shapes=[
            pltpu.VMEM((3, quarter, N2), jnp.bfloat16),
            pltpu.SemaphoreType.DMA((3,)),
        ],
        compiler_params=PARAMS,
        cost_estimate=cost(1000, 1000),
    )(projected, in_hbm(short_taps))
    rims = lax.ppermute(tails, "seq", [(s, s + 1) for s in range(seq_parts - 1)])
    started, heads, filter_here = pl.pallas_call(
        gate_kernel,
        out_shape=[
            jax.ShapeDtypeStruct((quarter, tok_len), jnp.bfloat16),
            jax.ShapeDtypeStruct((8, quarter), jnp.float32),
            jax.ShapeDtypeStruct((quarter, tok_len), jnp.bfloat16),
        ],
        in_specs=[whole(), whole(), anywhere],
        out_specs=[whole()] * 3,
        scratch_shapes=[pltpu.SemaphoreType.DMA],
        compiler_params=PARAMS,
        cost_estimate=cost(1000, 1000),
    )(pair, taps, in_hbm(long_filter))
    send = pl.pallas_call(
        mend_kernel,
        out_shape=jax.ShapeDtypeStruct((seq_parts, 2 * per_dev, tok_len), jnp.bfloat16),
        in_specs=[whole()] * 5,
        out_specs=anywhere,
        scratch_shapes=[
            pltpu.VMEM((seq_parts, per_dev, N2), jnp.bfloat16),
            pltpu.SemaphoreType.DMA((3,)),
        ],
        compiler_params=PARAMS,
        cost_estimate=cost(1000, 1000),
    )(started, taps, rims, heads, filter_here)
    received = transposed(send)
    query = pl.pallas_call(
        query_kernel,
        out_shape=jax.ShapeDtypeStruct((quarter, tok_len), jnp.bfloat16),
        in_specs=[anywhere, whole(), whole()],
        out_specs=whole(),
        scratch_shapes=[pltpu.VMEM((quarter, tok_len), jnp.bfloat16), pltpu.SemaphoreType.DMA],
        compiler_params=PARAMS,
        cost_estimate=cost(5_000_000, 1_000_000),
    )(projected, taps, rims)

    received, query = lax.optimization_barrier((received, query))

    own_skip = lax.dynamic_slice_in_dim(skip_gain, lax.axis_index("seq") * per_dev, per_dev, 0)
    own_skip = jnp.broadcast_to(own_skip[:, None], (per_dev, N2))
    response = pl.pallas_call(
        conv_kernel,
        out_shape=jax.ShapeDtypeStruct(chunk, jnp.bfloat16),
        in_specs=[whole()] * 7,
        out_specs=whole(),
        scratch_shapes=[
            pltpu.VMEM((seq_parts * (rows + GAP), N2), jnp.float32)
            for rows in (2 * per_dev, 2 * per_dev, per_dev, per_dev)
        ]
        + [pltpu.VMEM((per_dev * N1, 2 * N2), jnp.float32) for _ in range(2)],
        compiler_params=PARAMS,
        cost_estimate=cost(6_000_000_000, 4_000_000),
    )(received, own_skip, stage1, turns, forward2, inverse2, inverse1)
    returned = transposed(response)

    product = pl.pallas_call(
        product_kernel,
        out_shape=jax.ShapeDtypeStruct((tok_len, quarter), jnp.bfloat16),
        in_specs=[whole()] * 2,
        out_specs=whole(),
        compiler_params=PARAMS,
        cost_estimate=cost(1_000_000, 1_500_000),
    )(query, returned.reshape(quarter, tok_len))

    me = lax.axis_index("mp")
    to_far = [(m, m ^ 2) for m in range(4)]
    to_near = [(m, m ^ 1) for m in range(4)]

    far = lax.ppermute(product, "mp", to_far)
    near = lax.ppermute(product, "mp", to_near)
    out_len = w_out.shape[1]
    total, rest = pl.pallas_call(
        own_matmul_kernel,
        out_shape=[
            jax.ShapeDtypeStruct((tok_len, out_len), jnp.float32),
            jax.ShapeDtypeStruct((3 * quarter, out_len), jnp.bfloat16),
        ],
        in_specs=[whole(), anywhere],
        out_specs=[whole()] * 2,
        scratch_shapes=[pltpu.VMEM((quarter, out_len), jnp.bfloat16), pltpu.SemaphoreType.DMA((4,))],
        compiler_params=PARAMS,
        cost_estimate=cost(1000, 1000),
    )(product, in_hbm(w_out))
    total, rest, far = lax.optimization_barrier((total, rest, far))
    last = lax.ppermute(far, "mp", to_near)
    total = total + dot(far, rest[quarter : 2 * quarter])
    total = total + dot(near, rest[:quarter])
    return pl.pallas_call(
        last_matmul_kernel,
        out_shape=jax.ShapeDtypeStruct((tok_len, out_len), jnp.bfloat16),
        in_specs=[whole()] * 3,
        out_specs=anywhere,
        scratch_shapes=[
            pltpu.VMEM((tok_len, out_len), jnp.bfloat16),
            pltpu.SemaphoreType.DMA((4,)),
        ],
        compiler_params=PARAMS,
        cost_estimate=cost(500_000_000, 4_000_000),
    )(total, last, rest)


def solution(mesh):
    return jax.shard_map(
        per_device,
        mesh=mesh,
        in_specs=(
            P(None, "mp", "seq"),
            P(None, None, "mp"),
            P("mp", "seq"),
            P("mp"),
            P(None, "mp"),
        ),
        out_specs=P("seq", "mp"),
        check_vma=False,
    )
```
